32 devices in a mesh: fsdp: 8 (over y, x, core), dp: 4 (over z).
Axes of the slice: x: 2, y: 2, z: 4, core: 2. Of those that a mesh axis runs over, the one named last changes fastest.
Arguments:
- inputs: bfloat16 [16, 2048, 768], P('dp', 'fsdp'), may hold values from -6 to 6
- cotangent: bfloat16 [16, 2048, 768], P('dp', 'fsdp'), may hold values from -6 to 6
- segments: int32 [16, 2048], P('dp'), may hold values from 0 to 2047, as said below
- norm1_gain: bfloat16 [768], P('fsdp'), may hold values from 0.5 to 1.5
- norm1_bias: bfloat16 [768], P('fsdp'), may hold values from -1 to 1
- qkv_weight: bfloat16 [768, 2304], P('fsdp'), may hold values from -0.21875 to 0.21875
- query_bias: bfloat16 [768], P('fsdp'), may hold values from -1 to 1
- value_bias: bfloat16 [768], P('fsdp'), may hold values from -1 to 1
- proj_weight: bfloat16 [768, 768], P('fsdp'), may hold values from -1.25 to 1.25
- proj_bias: bfloat16 [768], P('fsdp'), may hold values from -1 to 1
- norm2_gain: bfloat16 [768], P('fsdp'), may hold values from 0.5 to 1.5
- norm2_bias: bfloat16 [768], P('fsdp'), may hold values from -1 to 1
- up_weight: bfloat16 [768, 3072], P('fsdp'), may hold values from -0.21875 to 0.21875
- up_bias: bfloat16 [3072], P('fsdp'), may hold values from -1 to 1
- down_weight: bfloat16 [3072, 768], P('fsdp'), may hold values from -0.109375 to 0.109375
- down_bias: bfloat16 [768], P('fsdp'), may hold values from -1 to 1
Outputs:
- layer_out: bfloat16 [16, 2048, 768], P('dp', 'fsdp')
- input_grad: float32 [16, 2048, 768], P('dp', 'fsdp')
- norm1_gain_grad: float32 [768], P('fsdp')
- norm1_bias_grad: float32 [768], P('fsdp')
- qkv_weight_grad: float32 [768, 2304], P('fsdp')
- query_bias_grad: float32 [768], P('fsdp')
- value_bias_grad: float32 [768], P('fsdp')
- proj_weight_grad: float32 [768, 768], P('fsdp')
- proj_bias_grad: float32 [768], P('fsdp')
- norm2_gain_grad: float32 [768], P('fsdp')
- norm2_bias_grad: float32 [768], P('fsdp')
- up_weight_grad: float32 [768, 3072], P('fsdp')
- up_bias_grad: float32 [3072], P('fsdp')
- down_weight_grad: float32 [3072, 768], P('fsdp')
- down_bias_grad: float32 [768], P('fsdp')
The draws below stay inside these ranges and needn't reach their ends.
Inputs may be any that keep to these rules, and one draw needn't show every extreme that they name: `segments`: along each sequence the document numbers never fall; tokens with equal numbers form one document, and each token's number is the position of its document's first token in the sequence; the last token of every sequence forms a document of its own. Among the 4 sequences of each index of dp one holds a document that begins within the first 256 tokens and ends within the last 256.
All inputs are finite; a program needn't handle non-finite values.
Results may differ from the reference program's by a relative error of at most 0.011.
Values may be sent and summed in bfloat16 or wider, within the bound.
A program may use at most 256 MiB of HBM per device.

```python
from functools import partial
import jax
import jax.numpy as jnp
from jax import lax

D = 768
H = 12
HD = 64
FF = 3072
LEN = 2048
SEQS = 4
TOK_SEQ = 256
NSEQ = 16


def draw_segments(key, part):
    flag_key, pick_key = jax.random.split(jax.random.fold_in(key, 17))
    position = jnp.arange(LEN, dtype=jnp.int32)
    starts = jax.random.randint(flag_key, (NSEQ, LEN), 0, max(LEN // 4, 2)) == 0
    chosen = jax.random.randint(pick_key, (NSEQ // SEQS,), 0, SEQS)
    sequence = jnp.arange(NSEQ, dtype=jnp.int32)
    spanning = sequence % SEQS == chosen[sequence // SEQS]
    inside = (position >= TOK_SEQ // 2) & (position < LEN - TOK_SEQ // 2)
    starts = starts & (position >= 1)[None, :] & jnp.logical_not(spanning[:, None] & inside[None, :])
    starts = starts | (position == LEN - 1)[None, :]
    first_places = jnp.where(starts, position[None, :], jnp.zeros((NSEQ, LEN), jnp.int32))
    return lax.cummax(first_places, axis=1).astype(jnp.int32)


def steps_of(key, extent, cuts, least, top_value):
    def one(axis_at, blocks):
        steps = jax.random.uniform(jax.random.fold_in(jax.random.fold_in(key, 6), axis_at), (blocks,), jnp.float32, least / len(cuts), top_value / len(cuts))
        return jnp.repeat(jnp.exp(steps), extent[axis_at] // blocks).reshape((-1,) + (1,) * (len(extent) - axis_at - 1))

    loudness = one(*cuts[0])
    for cut in cuts[1:]:
        loudness = loudness * one(*cut)
    return loudness


def normal_values(own_key, shape, scale, limit, shards=(), kind=jnp.bfloat16):
    entries = jax.random.normal(own_key, shape, jnp.float32) * scale
    if len(shards) > 0:
        entries = steps_of(own_key, shape, shards, -0.22, 0.18) * entries
    return jnp.clip(entries, min=-limit, max=limit).astype(kind)


def setup_inputs(seed: int = 0) -> dict:
    key_list = jax.random.split(jax.random.key(seed), 17)
    inputs = normal_values(key_list[0], (NSEQ, LEN, D), 1.0, 6.0, ((0, 4), (1, 8)))
    cotangent = normal_values(key_list[1], (NSEQ, LEN, D), 1.0, 6.0, ((0, 4), (1, 8)))
    segments = draw_segments(jax.random.fold_in(key_list[16], 71), 0)
    norm1_gain = jnp.clip(1.0 + 0.1 * jax.random.normal(key_list[3], (D,), jnp.float32), 0.5, 1.5).astype(jnp.bfloat16)
    norm1_bias = normal_values(key_list[4], (D,), 0.2, 1.0, ((0, 8),))
    qkv_weight = normal_values(key_list[5], (D, 3 * D), D ** -0.5, 0.21875, ((0, 8),))
    query_bias = normal_values(key_list[6], (D,), 0.2, 1.0, ((0, 8),))
    value_bias = normal_values(key_list[7], (D,), 0.2, 1.0, ((0, 8),))
    proj_weight = normal_values(key_list[8], (D, D), (D // 32) ** -0.5, 1.25, ((0, 8),))
    proj_bias = normal_values(key_list[9], (D,), 0.2, 1.0, ((0, 8),))
    norm2_gain = jnp.clip(1.0 + 0.1 * jax.random.normal(key_list[10], (D,), jnp.float32), 0.5, 1.5).astype(jnp.bfloat16)
    norm2_bias = normal_values(key_list[11], (D,), 0.2, 1.0, ((0, 8),))
    up_weight = normal_values(key_list[12], (D, FF), D ** -0.5, 0.21875, ((0, 8),))
    up_bias = normal_values(key_list[13], (FF,), 0.2, 1.0, ((0, 8),))
    down_weight = normal_values(key_list[14], (FF, D), FF ** -0.5, 0.109375, ((0, 8),))
    down_bias = normal_values(key_list[15], (D,), 0.2, 1.0, ((0, 8),))
    return dict(inputs=inputs, cotangent=cotangent, segments=segments, norm1_gain=norm1_gain, norm1_bias=norm1_bias, qkv_weight=qkv_weight, query_bias=query_bias, value_bias=value_bias, proj_weight=proj_weight, proj_bias=proj_bias, norm2_gain=norm2_gain, norm2_bias=norm2_bias, up_weight=up_weight, up_bias=up_bias, down_weight=down_weight, down_bias=down_bias)


@jax.custom_vjp
def low(v):
    return lax.optimization_barrier(v.astype(jnp.bfloat16)).astype(jnp.float32)

@jax.custom_vjp
def low_back(v):
    return v

def low_keep(v):
    return (low(v), None)

def low_pass(kept, grad):
    return (grad,)

def back_keep(v):
    return (v, None)

def back_low(kept, grad):
    return (low(grad),)
low.defvjp(low_keep, low_pass)
low_back.defvjp(back_keep, back_low)

def matmul(left_side, right_side):
    return jnp.dot(left_side, right_side, precision=lax.Precision.HIGHEST)

def layer_norm_core(values, gains, shifts):
    centre = lax.optimization_barrier(jnp.mean(values, axis=-1, keepdims=True))
    centred = values - centre
    spread = lax.optimization_barrier(jnp.mean(centred * centred, axis=-1, keepdims=True))
    return centred * lax.rsqrt(spread + 1e-05) * gains + shifts

def head_attention(visible, head_block):
    queries, keys_head, values_head = head_block
    raw_scores = low_back(matmul(queries, keys_head.T))
    scores = jnp.where(visible, raw_scores * HD ** (-0.5), -1e+30)
    highest = lax.optimization_barrier(jnp.max(scores, axis=-1, keepdims=True))
    weights = jnp.exp(scores - highest)
    probability = weights / lax.optimization_barrier(jnp.sum(weights, axis=-1, keepdims=True))
    return matmul(low(probability), values_head)

def forward(tokens_in, segment, params):
    gain_one, shift_one, qkv_full, query_shift, value_shift, proj_full, proj_shift, gain_two, shift_two, up_full, up_shift, down_full, down_shift = params
    normed_one = low(layer_norm_core(tokens_in, gain_one, shift_one))
    offsets = jnp.concatenate([query_shift, jnp.zeros_like(query_shift), value_shift])
    projected = low_back(low(matmul(normed_one, qkv_full) + offsets))
    split_heads = projected.reshape(LEN, 3, H, HD).transpose(1, 2, 0, 3)
    position = jnp.arange(LEN, dtype=jnp.int32)
    visible = (segment[:, None] == segment[None, :]) & (position[None, :] <= position[:, None])
    attend = jax.checkpoint(partial(head_attention, visible))
    contexts = lax.map(attend, (split_heads[0], split_heads[1], split_heads[2]))
    mixed = low_back(low(contexts.transpose(1, 0, 2).reshape(LEN, D)))
    residual = tokens_in + low_back(matmul(mixed, proj_full) + proj_shift)
    normed_two = low(layer_norm_core(residual, gain_two, shift_two))
    upward = low_back(matmul(normed_two, up_full) + up_shift)
    activated = low(jax.nn.gelu(upward, approximate=True))
    return residual + low_back(matmul(activated, down_full) + down_shift)

def reference(inputs, cotangent, segments, norm1_gain, norm1_bias, qkv_weight, query_bias, value_bias, proj_weight, proj_bias, norm2_gain, norm2_bias, up_weight, up_bias, down_weight, down_bias):
    params = tuple((weight.astype(jnp.float32) for weight in (norm1_gain, norm1_bias, qkv_weight, query_bias, value_bias, proj_weight, proj_bias, norm2_gain, norm2_bias, up_weight, up_bias, down_weight, down_bias)))

    def one_sequence(totals, sample):
        tokens_in, upstream, segment = sample
        outcome, pullback = jax.vjp(lambda tokens_arg, params_arg: forward(tokens_arg, segment, params_arg), tokens_in.astype(jnp.float32), params)
        token_grad, param_grads = pullback(upstream.astype(jnp.float32))
        totals = jax.tree.map(jnp.add, totals, param_grads)
        return (totals, (outcome.astype(jnp.bfloat16), token_grad))
    totals, (layer_out, input_grad) = lax.scan(one_sequence, jax.tree.map(jnp.zeros_like, params), (inputs, cotangent, segments))
    return (layer_out, input_grad, totals[0], totals[1], totals[2], totals[3], totals[4], totals[5], totals[6], totals[7], totals[8], totals[9], totals[10], totals[11], totals[12])
```

```python
from functools import partial

import jax
import jax.numpy as jnp
from jax import lax
from jax.experimental import pallas as pl
from jax.experimental.pallas import tpu as pltpu
from jax.sharding import PartitionSpec as P

HD = 64
PAIR = 2 * HD
FWD_BLOCK = 512
BWD_BLOCK = 512
HIDDEN = -1e30
NT = (((1,), (1,)), ((), ()))


def layer_norm_core(values, gains, shifts):
    centre = jnp.mean(values, axis=-1, keepdims=True)
    centred = values - centre
    spread = jnp.mean(centred * centred, axis=-1, keepdims=True)
    return centred * lax.rsqrt(spread + 1e-05) * gains + shifts


def smooth_gate(values):
    return jax.nn.gelu(values, approximate=True)


def head_masks(block):
    first = lax.broadcasted_iota(jnp.int32, block.shape, 1) < HD
    zero = jnp.zeros_like(block)
    return jnp.where(first, block, zero), jnp.where(first, zero, block)


def attend_kernel(size, start_ref, query_ref, key_ref, value_ref, context_ref, logsum_ref):
    row_block = pl.program_id(1)
    scaled = query_ref[...] * jnp.asarray(HD ** (-0.5), jnp.bfloat16)
    query_heads = head_masks(scaled)
    starts = start_ref[...]
    lane_first = lax.broadcasted_iota(jnp.int32, (size, PAIR), 1) < HD
    columns = lax.broadcasted_iota(jnp.int32, (size, size), 1)

    def step(block, carry, diagonal):
        begin = pl.multiple_of(block * size, size)
        keys = key_ref[pl.ds(begin, size), :]
        values = value_ref[pl.ds(begin, size), :]
        one = jnp.ones_like(values)
        value_heads = (
            jnp.where(lane_first, values, one),
            jnp.where(lane_first, one, values),
        )
        seen = columns >= starts - begin
        if diagonal:
            seen = seen & (columns <= lax.broadcasted_iota(jnp.int32, (size, size), 0))
        out = []
        for head in range(2):
            highest, total = carry[head]
            scores = lax.dot_general(
                query_heads[head], keys, NT, preferred_element_type=jnp.float32
            )
            scores = jnp.where(seen, scores, HIDDEN)
            now = jnp.maximum(highest, jnp.max(scores, axis=1, keepdims=True))
            weights = jnp.exp(scores - now).astype(jnp.bfloat16)
            total = total * jnp.exp(highest - now) + jnp.dot(
                weights, value_heads[head], preferred_element_type=jnp.float32
            )
            out.append((now, total))
        return tuple(out)

    fresh = (jnp.full((size, 1), HIDDEN, jnp.float32), jnp.zeros((size, PAIR), jnp.float32))
    carry = lax.fori_loop(0, row_block, lambda b, c: step(b, c, False), (fresh, fresh))
    (high_a, total_a), (high_b, total_b) = step(row_block, carry, True)
    sum_a = total_a[:, HD : HD + 1]
    sum_b = total_b[:, 0:1]
    context_ref[...] = jnp.where(lane_first, total_a / sum_a, total_b / sum_b).astype(
        context_ref.dtype
    )
    logsum_ref[...] = jnp.where(lane_first, high_a + jnp.log(sum_a), high_b + jnp.log(sum_b))


def attend(received, starts, pairs):
    length = received.shape[0]
    size = min(FWD_BLOCK, length)
    whole = lambda third: pl.BlockSpec((length, PAIR), lambda p, r, t=third: (0, t * pairs + p))
    block = pl.BlockSpec((size, PAIR), lambda p, r: (r, p))
    pair_work = length * length * PAIR * 4
    return pl.pallas_call(
        partial(attend_kernel, size),
        grid=(pairs, length // size),
        in_specs=[pl.BlockSpec((size, 1), lambda p, r: (r, 0)), block, whole(1), whole(2)],
        out_specs=[block, block],
        out_shape=[
            jax.ShapeDtypeStruct((length, pairs * PAIR), jnp.bfloat16),
            jax.ShapeDtypeStruct((length, pairs * PAIR), jnp.float32),
        ],
        cost_estimate=pl.CostEstimate(
            flops=pairs * pair_work * 4,
            bytes_accessed=received.size * 4,
            transcendentals=pairs * length * length,
        ),
        compiler_params=pltpu.CompilerParams(vmem_limit_bytes=48 * 1024 * 1024),
        name="attend",
    )(starts.reshape(length, 1), received, received, received)


def attend_back_kernel(
    size,
    start_ref,
    query_ref,
    key_ref,
    value_ref,
    grad_ref,
    context_ref,
    logsum_ref,
    out_ref,
    scaled_ref,
    lsum_ref,
    dots_ref,
    gradq_ref,
):
    key_block = pl.program_id(1)
    blocks = pl.num_programs(1)
    length = query_ref.shape[0]

    @pl.when(key_block == 0)
    def _():
        gradq_ref[...] = jnp.zeros_like(gradq_ref)
        scaled_ref[...] = query_ref[...] * jnp.asarray(HD ** (-0.5), jnp.bfloat16)

        def prepare(block, _):
            begin = pl.multiple_of(block * size, size)
            rows = pl.ds(begin, size)
            turned = logsum_ref[rows, :].T
            lsum_ref[0:1, rows] = turned[0:1, :]
            lsum_ref[1:2, rows] = turned[HD : HD + 1, :]
            product = (
                grad_ref[rows, :].astype(jnp.float32) * context_ref[rows, :].astype(jnp.float32)
            ).T
            dots_ref[0:1, rows] = jnp.sum(product[:HD, :], axis=0, keepdims=True)
            dots_ref[1:2, rows] = jnp.sum(product[HD:, :], axis=0, keepdims=True)
            return 0

        lax.fori_loop(0, blocks, prepare, 0)

    key_begin = pl.multiple_of(key_block * size, size)
    key_rows = pl.ds(key_begin, size)
    keys = key_ref[key_rows, :]
    values = value_ref[key_rows, :]
    turned_keys = keys.astype(jnp.float32).T.astype(jnp.bfloat16)
    top = lax.broadcasted_iota(jnp.int32, turned_keys.shape, 0) < HD
    none = jnp.zeros_like(turned_keys)
    turned_both = jnp.concatenate(
        [jnp.where(top, turned_keys, none), jnp.where(top, none, turned_keys)], axis=1
    )
    key_place = lax.broadcasted_iota(jnp.int32, (size, size), 0)

    def step(block, carry, diagonal):
        grad_key, grad_value = carry
        begin = pl.multiple_of(block * size, size)
        rows = pl.ds(begin, size)
        query_heads = head_masks(scaled_ref[rows, :])
        grad_heads = head_masks(grad_ref[rows, :])
        seen = key_place >= start_ref[0:1, rows] - key_begin
        if diagonal:
            seen = seen & (key_place <= lax.broadcasted_iota(jnp.int32, (size, size), 1))
        probs = []
        score_grads = []
        for head in range(2):
            scores = lax.dot_general(
                keys, query_heads[head], NT, preferred_element_type=jnp.float32
            )
            exact = jnp.exp(
                jnp.where(seen, scores - lsum_ref[head : head + 1, rows], HIDDEN)
            )
            prob_grad = lax.dot_general(
                values, grad_heads[head], NT, preferred_element_type=jnp.float32
            )
            probs.append(exact.astype(jnp.bfloat16))
            score_grads.append(
                (exact * (prob_grad - dots_ref[head : head + 1, rows])).astype(jnp.bfloat16)
            )
        grad_value = grad_value + jnp.dot(
            jnp.concatenate(probs, axis=1),
            jnp.concatenate(grad_heads, axis=0),
            preferred_element_type=jnp.float32,
        )
        grad_key = grad_key + jnp.dot(
            jnp.concatenate(score_grads, axis=1),
            jnp.concatenate(query_heads, axis=0),
            preferred_element_type=jnp.float32,
        )
        gradq_ref[:, rows] += jnp.dot(
            turned_both,
            jnp.concatenate(score_grads, axis=0),
            preferred_element_type=jnp.float32,
        )
        return grad_key, grad_value

    empty = jnp.zeros((size, PAIR), jnp.float32)
    carry = step(key_block, (empty, empty), True)
    grad_key, grad_value = lax.fori_loop(
        key_block + 1, blocks, lambda b, c: step(b, c, False), carry
    )
    out_ref[1, key_rows, :] = grad_key.astype(out_ref.dtype)
    out_ref[2, key_rows, :] = grad_value.astype(out_ref.dtype)

    @pl.when(key_block == blocks - 1)
    def _():
        def finish(block, _):
            rows = pl.ds(pl.multiple_of(block * size, size), size)
            out_ref[0, rows, :] = (gradq_ref[:, rows].T * HD ** (-0.5)).astype(out_ref.dtype)
            return 0

        lax.fori_loop(0, blocks, finish, 0)


def attend_back(received, starts, grad_context, context, logsum, pairs):
    length = received.shape[0]
    size = min(BWD_BLOCK, length)
    whole = lambda third: pl.BlockSpec((length, PAIR), lambda p, r, t=third: (0, t * pairs + p))
    pair_work = length * length * PAIR * 4
    return pl.pallas_call(
        partial(attend_back_kernel, size),
        grid=(pairs, length // size),
        in_specs=[
            pl.BlockSpec((1, length), lambda p, r: (0, 0)),
            whole(0),
            whole(1),
            whole(2),
            whole(0),
            whole(0),
            whole(0),
        ],
        out_specs=pl.BlockSpec((3, length, PAIR), lambda p, r: (0, 0, p)),
        out_shape=jax.ShapeDtypeStruct((3, length, pairs * PAIR), jnp.bfloat16),
        scratch_shapes=[
            pltpu.VMEM((length, PAIR), jnp.bfloat16),
            pltpu.VMEM((8, length), jnp.float32),
            pltpu.VMEM((8, length), jnp.float32),
            pltpu.VMEM((PAIR, length), jnp.float32),
        ],
        cost_estimate=pl.CostEstimate(
            flops=pairs * pair_work * 10,
            bytes_accessed=received.size * 8,
            transcendentals=pairs * length * length,
        ),
        compiler_params=pltpu.CompilerParams(vmem_limit_bytes=48 * 1024 * 1024),
        name="attend_back",
    )(starts.reshape(1, length), received, received, received, grad_context, context, logsum)


def local(
    inputs,
    cotangent,
    segments,
    norm1_gain,
    norm1_bias,
    qkv_weight,
    query_bias,
    value_bias,
    proj_weight,
    proj_bias,
    norm2_gain,
    norm2_bias,
    up_weight,
    up_bias,
    down_weight,
    down_bias,
    *,
    devices,
):
    seq_count, own_rows, model_width = inputs.shape
    length = segments.shape[1]
    token_count = seq_count * own_rows
    own_width = model_width // devices
    fold = up_bias.shape[0] // own_width
    groups = devices // seq_count
    pairs = -(-(model_width // PAIR) // groups)
    group_width = pairs * PAIR
    padded = groups * group_width
    place = lax.axis_index("fsdp")
    starts = lax.dynamic_slice_in_dim(segments, place // groups, 1, 0)

    def widen(block):
        spare = [(0, 0)] * (block.ndim - 1) + [(0, padded - model_width)]
        return jnp.pad(block, spare) if padded > model_width else block

    def to_heads(block):
        split = block.reshape(seq_count, own_rows, groups, -1).transpose(0, 2, 1, 3)
        split = split.reshape(devices, own_rows, -1)
        moved = lax.all_to_all(split, "fsdp", split_axis=0, concat_axis=0, tiled=True)
        return moved.reshape(length, -1)

    def by_group(block):
        thirds = widen(block.reshape(-1, 3, model_width))
        return (
            thirds.reshape(-1, 3, groups, group_width).transpose(0, 2, 1, 3).reshape(-1, 3 * padded)
        )

    small = jnp.concatenate(
        [
            jnp.stack(
                [
                    norm1_gain,
                    norm1_bias,
                    query_bias,
                    value_bias,
                    proj_bias,
                    norm2_gain,
                    norm2_bias,
                    down_bias,
                ]
            ),
            up_bias.reshape(fold, own_width),
        ]
    )
    small = jnp.pad(small, ((0, PAIR - small.shape[0]), (0, 0))).T
    first_full = lax.all_gather(
        jnp.concatenate([by_group(qkv_weight), small], axis=1), "fsdp", axis=0, tiled=True
    )
    qkv_full = first_full[:, : 3 * padded]
    vectors = first_full[:, 3 * padded :].T.astype(jnp.float32)
    gain_one, shift_one, query_shift, value_shift = vectors[0], vectors[1], vectors[2], vectors[3]
    proj_shift, gain_two, shift_two, down_shift = vectors[4], vectors[5], vectors[6], vectors[7]
    up_shift = (
        vectors[8 : 8 + fold].reshape(fold, devices, own_width).transpose(1, 0, 2).reshape(-1)
    )
    proj_full = lax.all_gather(proj_weight, "fsdp", axis=0, tiled=True)
    up_full = lax.all_gather(up_weight, "fsdp", axis=0, tiled=True)
    down_full = lax.all_gather(down_weight, "fsdp", axis=0, tiled=True)

    tokens_in = inputs.astype(jnp.float32).reshape(token_count, model_width)
    normed_one = layer_norm_core(tokens_in, gain_one, shift_one).astype(jnp.bfloat16)
    offsets = by_group(
        jnp.concatenate([query_shift, jnp.zeros_like(query_shift), value_shift])[None]
    )
    projected = (
        jnp.dot(normed_one, qkv_full, preferred_element_type=jnp.float32) + offsets
    ).astype(jnp.bfloat16)
    received = to_heads(projected)
    head_context, logsum = attend(received, starts, pairs)

    def to_tokens(block):
        moved = lax.all_to_all(
            block.reshape(devices, own_rows, -1), "fsdp", split_axis=0, concat_axis=0, tiled=True
        )
        moved = moved.reshape(seq_count, groups, own_rows, -1).transpose(0, 2, 1, 3)
        return moved.reshape(token_count, -1)

    mixed = to_tokens(head_context)[:, :model_width]
    attention_out = jnp.dot(mixed, proj_full, preferred_element_type=jnp.float32) + proj_shift
    residual = tokens_in + attention_out
    normed_two = layer_norm_core(residual, gain_two, shift_two).astype(jnp.bfloat16)
    upward = jnp.dot(normed_two, up_full, preferred_element_type=jnp.float32) + up_shift
    activated = smooth_gate(upward).astype(jnp.bfloat16)
    downward = jnp.dot(activated, down_full, preferred_element_type=jnp.float32) + down_shift
    layer_out = (residual + downward).astype(jnp.bfloat16)
    upstream = cotangent.astype(jnp.float32).reshape(token_count, model_width)
    down_grad = cotangent.reshape(token_count, model_width)

    def scatter(grad):
        return lax.psum_scatter(
            grad.astype(jnp.bfloat16), "fsdp", scatter_dimension=0, tiled=True
        )

    own_down = scatter(
        jnp.einsum("nf,nd->fd", activated, down_grad, preferred_element_type=jnp.float32)
    )
    grad_down_shift = jnp.sum(down_grad.astype(jnp.float32), axis=0)
    grad_activated = jnp.einsum(
        "nd,fd->nf", down_grad, down_full, preferred_element_type=jnp.float32
    )
    gate_value, gate_pullback = jax.vjp(smooth_gate, upward)
    up_grad = gate_pullback(grad_activated)[0].astype(jnp.bfloat16)
    own_up = scatter(
        jnp.einsum("nd,nf->df", normed_two, up_grad, preferred_element_type=jnp.float32)
    )
    grad_up_shift = jnp.sum(up_grad.astype(jnp.float32), axis=0)
    grad_normed_two = jnp.einsum("nf,df->nd", up_grad, up_full, preferred_element_type=jnp.float32)
    norm_value, norm_pullback = jax.vjp(layer_norm_core, residual, gain_two, shift_two)
    grad_residual_norm, grad_gain_two, grad_shift_two = norm_pullback(grad_normed_two)
    grad_residual = upstream + grad_residual_norm
    attention_grad = grad_residual.astype(jnp.bfloat16)
    own_proj = scatter(
        jnp.einsum("nd,ne->de", mixed, attention_grad, preferred_element_type=jnp.float32)
    )
    grad_proj_shift = jnp.sum(attention_grad.astype(jnp.float32), axis=0)
    grad_mixed = jnp.einsum(
        "ne,de->nd", attention_grad, proj_full, preferred_element_type=jnp.float32
    ).astype(jnp.bfloat16)
    head_grads = attend_back(
        received, starts, to_heads(widen(grad_mixed)), head_context, logsum, pairs
    )
    moved = lax.all_to_all(
        head_grads.reshape(3, devices, own_rows, group_width),
        "fsdp",
        split_axis=1,
        concat_axis=1,
        tiled=True,
    ).reshape(3, seq_count, groups, own_rows, group_width)
    qkv_grad = moved.transpose(1, 3, 2, 0, 4).reshape(token_count, 3 * padded)
    grad_qkv_weight = jnp.einsum(
        "nd,ne->de", normed_one, qkv_grad, preferred_element_type=jnp.float32
    )
    column_sums = jnp.sum(qkv_grad.astype(jnp.float32), axis=0)
    column_sums = column_sums.reshape(groups, 3, group_width).transpose(1, 0, 2)
    column_sums = column_sums.reshape(3, padded)[:, :model_width]
    grad_normed_one = jnp.einsum(
        "ne,de->nd", qkv_grad, qkv_full, preferred_element_type=jnp.float32
    )
    first_value, first_pullback = jax.vjp(layer_norm_core, tokens_in, gain_one, shift_one)
    grad_input_norm, grad_gain_one, grad_shift_one = first_pullback(grad_normed_one)
    input_grad = grad_residual + grad_input_norm
    early = lax.psum((own_proj, own_up, own_down), "dp")
    small_grads = jnp.concatenate(
        [
            jnp.stack(
                [
                    grad_gain_one,
                    grad_shift_one,
                    column_sums[0],
                    column_sums[2],
                    grad_proj_shift,
                    grad_gain_two,
                    grad_shift_two,
                    grad_down_shift,
                ]
            ),
            grad_up_shift.reshape(devices, fold, own_width)
            .transpose(1, 0, 2)
            .reshape(fold, model_width),
        ]
    )
    small_grads = jnp.pad(small_grads, ((0, PAIR - small_grads.shape[0]), (0, 0))).T
    last = scatter(jnp.concatenate([grad_qkv_weight, small_grads], axis=1))
    last, early = lax.optimization_barrier((last, early))
    last = lax.psum(last, "dp").astype(jnp.float32)
    sum_proj, sum_up, sum_down = (part.astype(jnp.float32) for part in early)
    sum_qkv = last[:, : 3 * padded].reshape(own_width, groups, 3, group_width)
    sum_qkv = sum_qkv.transpose(0, 2, 1, 3).reshape(own_width, 3, padded)[:, :, :model_width]
    sum_qkv = sum_qkv.reshape(own_width, 3 * model_width)
    own = last[:, 3 * padded :].T
    return (
        layer_out.reshape(seq_count, own_rows, model_width),
        input_grad.reshape(seq_count, own_rows, model_width),
        own[0],
        own[1],
        sum_qkv,
        own[2],
        own[3],
        sum_proj,
        own[4],
        own[5],
        own[6],
        sum_up,
        own[8 : 8 + fold].reshape(-1),
        sum_down,
        own[7],
    )


def solution(mesh):
    in_specs = (
        P("dp", "fsdp", None),
        P("dp", "fsdp", None),
        P("dp", None),
        P("fsdp"),
        P("fsdp"),
        P("fsdp", None),
        P("fsdp"),
        P("fsdp"),
        P("fsdp", None),
        P("fsdp"),
        P("fsdp"),
        P("fsdp"),
        P("fsdp", None),
        P("fsdp"),
        P("fsdp", None),
        P("fsdp"),
    )
    out_specs = (
        P("dp", "fsdp", None),
        P("dp", "fsdp", None),
        P("fsdp"),
        P("fsdp"),
        P("fsdp", None),
        P("fsdp"),
        P("fsdp"),
        P("fsdp", None),
        P("fsdp"),
        P("fsdp"),
        P("fsdp"),
        P("fsdp", None),
        P("fsdp"),
        P("fsdp", None),
        P("fsdp"),
    )
    return jax.shard_map(
        partial(local, devices=mesh.shape["fsdp"]),
        mesh=mesh, in_specs=in_specs, out_specs=out_specs, check_vma=False,
    )
```

```python
from functools import partial

import jax
import jax.numpy as jnp
from jax import lax
from jax.experimental import pallas as pl
from jax.experimental.pallas import tpu as pltpu
from jax.sharding import PartitionSpec as P

HD = 64
PAIR = 2 * HD
FWD_BLOCK = 512
BWD_BLOCK = 512
HIDDEN = -1e30
NT = (((1,), (1,)), ((), ()))


def layer_norm_core(values, gains, shifts):
    centre = jnp.mean(values, axis=-1, keepdims=True)
    centred = values - centre
    spread = jnp.mean(centred * centred, axis=-1, keepdims=True)
    return centred * lax.rsqrt(spread + 1e-05) * gains + shifts


def smooth_gate(values):
    return jax.nn.gelu(values, approximate=True)


def head_masks(block):
    first = lax.broadcasted_iota(jnp.int32, block.shape, 1) < HD
    zero = jnp.zeros_like(block)
    return jnp.where(first, block, zero), jnp.where(first, zero, block)


def attend_kernel(size, start_ref, query_ref, key_ref, value_ref, context_ref, logsum_ref):
    row_block = pl.program_id(1)
    scaled = query_ref[...] * jnp.asarray(HD ** (-0.5), jnp.bfloat16)
    query_heads = head_masks(scaled)
    starts = start_ref[...]
    lane_first = lax.broadcasted_iota(jnp.int32, (size, PAIR), 1) < HD
    columns = lax.broadcasted_iota(jnp.int32, (size, size), 1)

    def step(block, carry, diagonal):
        begin = pl.multiple_of(block * size, size)
        keys = key_ref[pl.ds(begin, size), :]
        values = value_ref[pl.ds(begin, size), :]
        one = jnp.ones_like(values)
        value_heads = (
            jnp.where(lane_first, values, one),
            jnp.where(lane_first, one, values),
        )
        seen = columns >= starts - begin
        if diagonal:
            seen = seen & (columns <= lax.broadcasted_iota(jnp.int32, (size, size), 0))
        out = []
        for head in range(2):
            highest, total = carry[head]
            scores = lax.dot_general(
                query_heads[head], keys, NT, preferred_element_type=jnp.float32
            )
            scores = jnp.where(seen, scores, HIDDEN)
            now = jnp.maximum(highest, jnp.max(scores, axis=1, keepdims=True))
            weights = jnp.exp(scores - now).astype(jnp.bfloat16)
            total = total * jnp.exp(highest - now) + jnp.dot(
                weights, value_heads[head], preferred_element_type=jnp.float32
            )
            out.append((now, total))
        return tuple(out)

    fresh = (jnp.full((size, 1), HIDDEN, jnp.float32), jnp.zeros((size, PAIR), jnp.float32))
    carry = lax.fori_loop(0, row_block, lambda b, c: step(b, c, False), (fresh, fresh))
    (high_a, total_a), (high_b, total_b) = step(row_block, carry, True)
    sum_a = total_a[:, HD : HD + 1]
    sum_b = total_b[:, 0:1]
    context_ref[...] = jnp.where(lane_first, total_a / sum_a, total_b / sum_b).astype(
        context_ref.dtype
    )
    logsum_ref[...] = jnp.where(lane_first, high_a + jnp.log(sum_a), high_b + jnp.log(sum_b))


def attend(received, starts, pairs):
    length = received.shape[0]
    size = min(FWD_BLOCK, length)
    whole = lambda third: pl.BlockSpec((length, PAIR), lambda p, r, t=third: (0, t * pairs + p))
    block = pl.BlockSpec((size, PAIR), lambda p, r: (r, p))
    pair_work = length * length * PAIR * 4
    return pl.pallas_call(
        partial(attend_kernel, size),
        grid=(pairs, length // size),
        in_specs=[pl.BlockSpec((size, 1), lambda p, r: (r, 0)), block, whole(1), whole(2)],
        out_specs=[block, block],
        out_shape=[
            jax.ShapeDtypeStruct((length, pairs * PAIR), jnp.bfloat16),
            jax.ShapeDtypeStruct((length, pairs * PAIR), jnp.float32),
        ],
        cost_estimate=pl.CostEstimate(
            flops=pairs * pair_work * 4,
            bytes_accessed=received.size * 4,
            transcendentals=pairs * length * length,
        ),
        compiler_params=pltpu.CompilerParams(vmem_limit_bytes=48 * 1024 * 1024),
        name="attend",
    )(starts.reshape(length, 1), received, received, received)


def attend_back_kernel(
    size,
    start_ref,
    query_ref,
    key_ref,
    value_ref,
    grad_ref,
    context_ref,
    logsum_ref,
    out_ref,
    scaled_ref,
    lsum_ref,
    dots_ref,
    gradq_ref,
):
    key_block = pl.program_id(1)
    blocks = pl.num_programs(1)
    length = query_ref.shape[0]

    @pl.when(key_block == 0)
    def _():
        gradq_ref[...] = jnp.zeros_like(gradq_ref)
        scaled_ref[...] = query_ref[...] * jnp.asarray(HD ** (-0.5), jnp.bfloat16)

        def prepare(block, _):
            begin = pl.multiple_of(block * size, size)
            rows = pl.ds(begin, size)
            turned = logsum_ref[rows, :].T
            lsum_ref[0:1, rows] = turned[0:1, :]
            lsum_ref[1:2, rows] = turned[HD : HD + 1, :]
            product = (
                grad_ref[rows, :].astype(jnp.float32) * context_ref[rows, :].astype(jnp.float32)
            ).T
            dots_ref[0:1, rows] = jnp.sum(product[:HD, :], axis=0, keepdims=True)
            dots_ref[1:2, rows] = jnp.sum(product[HD:, :], axis=0, keepdims=True)
            return 0

        lax.fori_loop(0, blocks, prepare, 0)

    key_begin = pl.multiple_of(key_block * size, size)
    key_rows = pl.ds(key_begin, size)
    keys = key_ref[key_rows, :]
    values = value_ref[key_rows, :]
    turned_keys = keys.astype(jnp.float32).T.astype(jnp.bfloat16)
    top = lax.broadcasted_iota(jnp.int32, turned_keys.shape, 0) < HD
    none = jnp.zeros_like(turned_keys)
    turned_both = jnp.concatenate(
        [jnp.where(top, turned_keys, none), jnp.where(top, none, turned_keys)], axis=1
    )
    key_place = lax.broadcasted_iota(jnp.int32, (size, size), 0)

    def step(block, carry, diagonal):
        grad_key, grad_value = carry
        begin = pl.multiple_of(block * size, size)
        rows = pl.ds(begin, size)
        query_heads = head_masks(scaled_ref[rows, :])
        grad_heads = head_masks(grad_ref[rows, :])
        seen = key_place >= start_ref[0:1, rows] - key_begin
        if diagonal:
            seen = seen & (key_place <= lax.broadcasted_iota(jnp.int32, (size, size), 1))
        probs = []
        score_grads = []
        for head in range(2):
            scores = lax.dot_general(
                keys, query_heads[head], NT, preferred_element_type=jnp.float32
            )
            exact = jnp.exp(
                jnp.where(seen, scores - lsum_ref[head : head + 1, rows], HIDDEN)
            )
            prob_grad = lax.dot_general(
                values, grad_heads[head], NT, preferred_element_type=jnp.float32
            )
            probs.append(exact.astype(jnp.bfloat16))
            score_grads.append(
                (exact * (prob_grad - dots_ref[head : head + 1, rows])).astype(jnp.bfloat16)
            )
        grad_value = grad_value + jnp.dot(
            jnp.concatenate(probs, axis=1),
            jnp.concatenate(grad_heads, axis=0),
            preferred_element_type=jnp.float32,
        )
        grad_key = grad_key + jnp.dot(
            jnp.concatenate(score_grads, axis=1),
            jnp.concatenate(query_heads, axis=0),
            preferred_element_type=jnp.float32,
        )
        gradq_ref[:, rows] += jnp.dot(
            turned_both,
            jnp.concatenate(score_grads, axis=0),
            preferred_element_type=jnp.float32,
        )
        return grad_key, grad_value

    empty = jnp.zeros((size, PAIR), jnp.float32)
    carry = step(key_block, (empty, empty), True)
    grad_key, grad_value = lax.fori_loop(
        key_block + 1, blocks, lambda b, c: step(b, c, False), carry
    )
    out_ref[1, key_rows, :] = grad_key.astype(out_ref.dtype)
    out_ref[2, key_rows, :] = grad_value.astype(out_ref.dtype)

    @pl.when(key_block == blocks - 1)
    def _():
        def finish(block, _):
            rows = pl.ds(pl.multiple_of(block * size, size), size)
            out_ref[0, rows, :] = (gradq_ref[:, rows].T * HD ** (-0.5)).astype(out_ref.dtype)
            return 0

        lax.fori_loop(0, blocks, finish, 0)


def attend_back(received, starts, grad_context, context, logsum, pairs):
    length = received.shape[0]
    size = min(BWD_BLOCK, length)
    whole = lambda third: pl.BlockSpec((length, PAIR), lambda p, r, t=third: (0, t * pairs + p))
    pair_work = length * length * PAIR * 4
    return pl.pallas_call(
        partial(attend_back_kernel, size),
        grid=(pairs, length // size),
        in_specs=[
            pl.BlockSpec((1, length), lambda p, r: (0, 0)),
            whole(0),
            whole(1),
            whole(2),
            whole(0),
            whole(0),
            whole(0),
        ],
        out_specs=pl.BlockSpec((3, length, PAIR), lambda p, r: (0, 0, p)),
        out_shape=jax.ShapeDtypeStruct((3, length, pairs * PAIR), jnp.bfloat16),
        scratch_shapes=[
            pltpu.VMEM((length, PAIR), jnp.bfloat16),
            pltpu.VMEM((8, length), jnp.float32),
            pltpu.VMEM((8, length), jnp.float32),
            pltpu.VMEM((PAIR, length), jnp.float32),
        ],
        cost_estimate=pl.CostEstimate(
            flops=pairs * pair_work * 10,
            bytes_accessed=received.size * 8,
            transcendentals=pairs * length * length,
        ),
        compiler_params=pltpu.CompilerParams(vmem_limit_bytes=48 * 1024 * 1024),
        name="attend_back",
    )(starts.reshape(1, length), received, received, received, grad_context, context, logsum)


def local(
    inputs,
    cotangent,
    segments,
    norm1_gain,
    norm1_bias,
    qkv_weight,
    query_bias,
    value_bias,
    proj_weight,
    proj_bias,
    norm2_gain,
    norm2_bias,
    up_weight,
    up_bias,
    down_weight,
    down_bias,
    *,
    devices,
):
    seq_count, own_rows, model_width = inputs.shape
    length = segments.shape[1]
    token_count = seq_count * own_rows
    own_width = model_width // devices
    fold = up_bias.shape[0] // own_width
    groups = devices // seq_count
    pairs = -(-(model_width // PAIR) // groups)
    group_width = pairs * PAIR
    padded = groups * group_width
    place = lax.axis_index("fsdp")
    starts = lax.dynamic_slice_in_dim(segments, place // groups, 1, 0)

    def widen(block):
        spare = [(0, 0)] * (block.ndim - 1) + [(0, padded - model_width)]
        return jnp.pad(block, spare) if padded > model_width else block

    def to_heads(block):
        split = block.reshape(seq_count, own_rows, groups, -1).transpose(0, 2, 1, 3)
        split = split.reshape(devices, own_rows, -1)
        moved = lax.all_to_all(split, "fsdp", split_axis=0, concat_axis=0, tiled=True)
        return moved.reshape(length, -1)

    def by_group(block):
        thirds = widen(block.reshape(-1, 3, model_width))
        return (
            thirds.reshape(-1, 3, groups, group_width).transpose(0, 2, 1, 3).reshape(-1, 3 * padded)
        )

    small = jnp.concatenate(
        [
            jnp.stack(
                [
                    norm1_gain,
                    norm1_bias,
                    query_bias,
                    value_bias,
                    proj_bias,
                    norm2_gain,
                    norm2_bias,
                    down_bias,
                ]
            ),
            up_bias.reshape(fold, own_width),
        ]
    )
    small = jnp.pad(small, ((0, PAIR - small.shape[0]), (0, 0))).T
    first_full = lax.all_gather(
        jnp.concatenate([by_group(qkv_weight), small], axis=1), "fsdp", axis=0, tiled=True
    )
    qkv_full = first_full[:, : 3 * padded]
    vectors = first_full[:, 3 * padded :].T.astype(jnp.float32)
    gain_one, shift_one, query_shift, value_shift = vectors[0], vectors[1], vectors[2], vectors[3]
    proj_shift, gain_two, shift_two, down_shift = vectors[4], vectors[5], vectors[6], vectors[7]
    up_shift = (
        vectors[8 : 8 + fold].reshape(fold, devices, own_width).transpose(1, 0, 2).reshape(-1)
    )
    proj_full = lax.all_gather(proj_weight, "fsdp", axis=0, tiled=True)
    up_full = lax.all_gather(up_weight, "fsdp", axis=0, tiled=True)
    down_full = lax.all_gather(down_weight, "fsdp", axis=0, tiled=True)

    tokens_in = inputs.astype(jnp.float32).reshape(token_count, model_width)
    normed_one = layer_norm_core(tokens_in, gain_one, shift_one).astype(jnp.bfloat16)
    offsets = by_group(
        jnp.concatenate([query_shift, jnp.zeros_like(query_shift), value_shift])[None]
    )
    projected = (
        jnp.dot(normed_one, qkv_full, preferred_element_type=jnp.float32) + offsets
    ).astype(jnp.bfloat16)
    received = to_heads(projected)
    head_context, logsum = attend(received, starts, pairs)

    def to_tokens(block):
        moved = lax.all_to_all(
            block.reshape(devices, own_rows, -1), "fsdp", split_axis=0, concat_axis=0, tiled=True
        )
        moved = moved.reshape(seq_count, groups, own_rows, -1).transpose(0, 2, 1, 3)
        return moved.reshape(token_count, -1)

    mixed = to_tokens(head_context)[:, :model_width]
    attention_out = jnp.dot(mixed, proj_full, preferred_element_type=jnp.float32) + proj_shift
    residual = tokens_in + attention_out
    normed_two = layer_norm_core(residual, gain_two, shift_two).astype(jnp.bfloat16)
    upward = jnp.dot(normed_two, up_full, preferred_element_type=jnp.float32) + up_shift
    activated = smooth_gate(upward).astype(jnp.bfloat16)
    downward = jnp.dot(activated, down_full, preferred_element_type=jnp.float32) + down_shift
    layer_out = (residual + downward).astype(jnp.bfloat16)
    upstream = cotangent.astype(jnp.float32).reshape(token_count, model_width)
    down_grad = cotangent.reshape(token_count, model_width)

    def scatter(grad):
        return lax.psum_scatter(
            grad.astype(jnp.bfloat16), "fsdp", scatter_dimension=0, tiled=True
        )

    own_down = scatter(
        jnp.einsum("nf,nd->fd", activated, down_grad, preferred_element_type=jnp.float32)
    )
    grad_down_shift = jnp.sum(down_grad.astype(jnp.float32), axis=0)
    grad_activated = jnp.einsum(
        "nd,fd->nf", down_grad, down_full, preferred_element_type=jnp.float32
    )
    gate_value, gate_pullback = jax.vjp(smooth_gate, upward)
    up_grad = gate_pullback(grad_activated)[0].astype(jnp.bfloat16)
    own_up = scatter(
        jnp.einsum("nd,nf->df", normed_two, up_grad, preferred_element_type=jnp.float32)
    )
    grad_up_shift = jnp.sum(up_grad.astype(jnp.float32), axis=0)
    grad_normed_two = jnp.einsum("nf,df->nd", up_grad, up_full, preferred_element_type=jnp.float32)
    norm_value, norm_pullback = jax.vjp(layer_norm_core, residual, gain_two, shift_two)
    grad_residual_norm, grad_gain_two, grad_shift_two = norm_pullback(grad_normed_two)
    grad_residual = upstream + grad_residual_norm
    attention_grad = grad_residual.astype(jnp.bfloat16)
    own_proj = scatter(
        jnp.einsum("nd,ne->de", mixed, attention_grad, preferred_element_type=jnp.float32)
    )
    grad_proj_shift = jnp.sum(attention_grad.astype(jnp.float32), axis=0)
    grad_mixed = jnp.einsum(
        "ne,de->nd", attention_grad, proj_full, preferred_element_type=jnp.float32
    ).astype(jnp.bfloat16)
    head_grads = attend_back(
        received, starts, to_heads(widen(grad_mixed)), head_context, logsum, pairs
    )
    moved = lax.all_to_all(
        head_grads.reshape(3, devices, own_rows, group_width),
        "fsdp",
        split_axis=1,
        concat_axis=1,
        tiled=True,
    ).reshape(3, seq_count, groups, own_rows, group_width)
    qkv_grad = moved.transpose(1, 3, 2, 0, 4).reshape(token_count, 3 * padded)
    grad_qkv_weight = jnp.einsum(
        "nd,ne->de", normed_one, qkv_grad, preferred_element_type=jnp.float32
    )
    column_sums = jnp.sum(qkv_grad.astype(jnp.float32), axis=0)
    column_sums = column_sums.reshape(groups, 3, group_width).transpose(1, 0, 2)
    column_sums = column_sums.reshape(3, padded)[:, :model_width]
    grad_normed_one = jnp.einsum(
        "ne,de->nd", qkv_grad, qkv_full, preferred_element_type=jnp.float32
    )
    first_value, first_pullback = jax.vjp(layer_norm_core, tokens_in, gain_one, shift_one)
    grad_input_norm, grad_gain_one, grad_shift_one = first_pullback(grad_normed_one)
    input_grad = grad_residual + grad_input_norm
    small_grads = jnp.concatenate(
        [
            jnp.stack(
                [
                    grad_gain_one,
                    grad_shift_one,
                    column_sums[0],
                    column_sums[2],
                    grad_proj_shift,
                    grad_gain_two,
                    grad_shift_two,
                    grad_down_shift,
                ]
            ),
            grad_up_shift.reshape(devices, fold, own_width)
            .transpose(1, 0, 2)
            .reshape(fold, model_width),
        ]
    )
    small_grads = jnp.pad(small_grads, ((0, PAIR - small_grads.shape[0]), (0, 0))).T
    last = scatter(jnp.concatenate([grad_qkv_weight, small_grads], axis=1))
    last, sum_proj, sum_up, sum_down = (
        part.astype(jnp.float32) for part in lax.psum((last, own_proj, own_up, own_down), "dp")
    )
    sum_qkv = last[:, : 3 * padded].reshape(own_width, groups, 3, group_width)
    sum_qkv = sum_qkv.transpose(0, 2, 1, 3).reshape(own_width, 3, padded)[:, :, :model_width]
    sum_qkv = sum_qkv.reshape(own_width, 3 * model_width)
    own = last[:, 3 * padded :].T
    return (
        layer_out.reshape(seq_count, own_rows, model_width),
        input_grad.reshape(seq_count, own_rows, model_width),
        own[0],
        own[1],
        sum_qkv,
        own[2],
        own[3],
        sum_proj,
        own[4],
        own[5],
        own[6],
        sum_up,
        own[8 : 8 + fold].reshape(-1),
        sum_down,
        own[7],
    )


def solution(mesh):
    in_specs = (
        P("dp", "fsdp", None),
        P("dp", "fsdp", None),
        P("dp", None),
        P("fsdp"),
        P("fsdp"),
        P("fsdp", None),
        P("fsdp"),
        P("fsdp"),
        P("fsdp", None),
        P("fsdp"),
        P("fsdp"),
        P("fsdp"),
        P("fsdp", None),
        P("fsdp"),
        P("fsdp", None),
        P("fsdp"),
    )
    out_specs = (
        P("dp", "fsdp", None),
        P("dp", "fsdp", None),
        P("fsdp"),
        P("fsdp"),
        P("fsdp", None),
        P("fsdp"),
        P("fsdp"),
        P("fsdp", None),
        P("fsdp"),
        P("fsdp"),
        P("fsdp"),
        P("fsdp", None),
        P("fsdp"),
        P("fsdp", None),
        P("fsdp"),
    )
    return jax.shard_map(
        partial(local, devices=mesh.shape["fsdp"]),
        mesh=mesh, in_specs=in_specs, out_specs=out_specs, check_vma=False,
    )
```
